256 devices in a mesh: row: 64 (over z, x, y_lo), col: 4 (over y_hi, core).
Axes of the slice: x: 4, y: 4 (y_hi: 2, y_lo: 2; y = y_hi * 2 + y_lo), z: 8, core: 2. Of those that a mesh axis runs over, the one named last changes fastest.
Arguments:
- pair: bfloat16 [1024, 1024, 128], P('row', 'col'), may hold values from -6 to 6
- w_in: bfloat16 [2, 128, 512], replicated, may hold values from -0.5 to 0.5
- w_gate: bfloat16 [2, 128, 128], replicated, may hold values from -0.5 to 0.5
- w_out: bfloat16 [2, 128, 128], replicated, may hold values from -0.5 to 0.5
Outputs:
- pair_out: bfloat16 [1024, 1024, 128], P('row', 'col')
The draws below stay inside these ranges and needn't reach their ends.
All inputs are finite; a program needn't handle non-finite values.
Results may differ from the reference program's by a relative error of at most 0.018.
Values may be sent and summed in bfloat16 or wider, within the bound.
No kernel may reach another device: no remote copies, remote signals or barrier semaphores. Data moves between devices by JAX's collectives and lax.ppermute only.
A program may use at most 64 MiB of HBM per device.

```python
import jax
import jax.numpy as jnp
from jax import lax

C = 128
H = 128
ROWS_DEV = 16
RES = 1024
N_ROW = 64


def levels(rng, dims, split, low, top_value):
    loudness, own = 1.0, jax.random.fold_in(rng, 6)
    for axis_at, blocks in split:
        steps = jnp.exp(jax.random.uniform(jax.random.fold_in(own, axis_at), (blocks,), jnp.float32, low / len(split), top_value / len(split)))
        loudness = loudness * jnp.repeat(steps, dims[axis_at] // blocks).reshape([-1 if axis == axis_at else 1 for axis in range(len(dims))])
    return loudness


def normal_values(rng, dims, scale, most, shards=(), held_as=jnp.bfloat16):
    result = scale * jax.random.normal(rng, dims, jnp.float32)
    if shards:
        result = result * levels(rng, dims, shards, -0.22, 0.18)
    return jnp.clip(result, -most, most).astype(held_as)


def setup_inputs(seed: int = 0) -> dict:
    splits = jax.random.split(jax.random.key(seed), 5)
    pair = normal_values(splits[0], (RES, RES, C), 1.0, 6.0, ((0, 64), (1, 4)))
    w_in = normal_values(splits[1], (2, C, 4 * H), C ** -0.5, 0.5)
    w_gate = normal_values(splits[2], (2, C, C), C ** -0.5, 0.5)
    w_out = normal_values(splits[3], (2, H, C), H ** -0.5, 0.5)
    return dict(pair=pair, w_in=w_in, w_gate=w_gate, w_out=w_out)


def layer_norm(value, axis):
    mean = lax.optimization_barrier(jnp.mean(value, axis=axis, keepdims=True))
    centred = value - mean
    var = lax.optimization_barrier(jnp.mean(centred * centred, axis=axis, keepdims=True))
    return centred * lax.rsqrt(var + 1e-05)

def reference(pair, w_in, w_gate, w_out):
    hidden = w_out.shape[1]
    width = pair.shape[2]
    for layer in range(2):
        blocks = pair.reshape(N_ROW, ROWS_DEV, RES, width)
        weights_in = w_in[layer].astype(jnp.float32)
        weights_gate = w_gate[layer].astype(jnp.float32)
        weights_out = w_out[layer].astype(jnp.float32)

        def project(block):
            normed = layer_norm(block.astype(jnp.float32), -1).astype(jnp.bfloat16)
            proj = jnp.einsum('ijd,de->ije', normed.astype(jnp.float32), weights_in)
            left = (jax.nn.sigmoid(proj[..., hidden:2 * hidden]) * proj[..., :hidden]).astype(jnp.bfloat16)
            right = (jax.nn.sigmoid(proj[..., 3 * hidden:]) * proj[..., 2 * hidden:3 * hidden]).astype(jnp.bfloat16)
            return (left, right)
        left, right = lax.map(project, blocks)
        left_major = jnp.moveaxis(left.reshape(RES, RES, hidden), 2, 0)
        right_major = jnp.moveaxis(right.reshape(RES, RES, hidden), 2, 0)
        if layer == 0:

            def contract(operands):
                return jnp.dot(operands[0], operands[1].T, preferred_element_type=jnp.float32).astype(jnp.bfloat16)
        else:

            def contract(operands):
                return jnp.dot(operands[0].T, operands[1], preferred_element_type=jnp.float32).astype(jnp.bfloat16)
        triangle = lax.map(contract, (left_major, right_major))
        triangle = jnp.moveaxis(triangle, 0, 2).reshape(N_ROW, ROWS_DEV, RES, hidden)

        def finish(operands):
            block, tri_block = operands
            normed = layer_norm(block.astype(jnp.float32), -1).astype(jnp.bfloat16)
            summed = layer_norm(tri_block.astype(jnp.float32), -1).astype(jnp.bfloat16)
            gate = jax.nn.sigmoid(jnp.einsum('ijd,de->ije', normed.astype(jnp.float32), weights_gate))
            update = gate * jnp.einsum('ijh,hd->ijd', summed.astype(jnp.float32), weights_out)
            return (block.astype(jnp.float32) + update).astype(jnp.bfloat16)
        pair = lax.map(finish, (blocks, triangle)).reshape(RES, RES, width)
    return pair
```

```python
import functools

import jax
import jax.numpy as jnp
from jax import lax
from jax.experimental import pallas as pl
from jax.experimental.pallas import tpu as pltpu
from jax.sharding import Mesh, PartitionSpec as P

AXES = ("z", "x", "yl", "yh", "core")
CHIPS = ("z", "x", "yl", "yh")
F32, BF16 = jnp.float32, jnp.bfloat16
VMEM = pl.BlockSpec(memory_space=pltpu.VMEM)
SMEM = pl.BlockSpec(memory_space=pltpu.SMEM)


def params():
    return pltpu.CompilerParams(vmem_limit_bytes=48 * 1024 * 1024)


def sigmoid(v):
    return 0.5 * jnp.tanh(0.5 * v) + 0.5


def norm(v):
    mean = jnp.mean(v, axis=0, keepdims=True)
    centred = v - mean
    var = jnp.mean(centred * centred, axis=0, keepdims=True)
    return centred * lax.rsqrt(var + 1e-05)


def turned(w):
    return w.astype(F32).T.astype(BF16)


def dot(a, b):
    return jnp.dot(a, b, preferred_element_type=F32)


def project(x, w_t, r, rows, wide, hidden):
    proj = dot(w_t, x)
    left = sigmoid(proj[hidden : 2 * hidden]) * proj[:hidden]
    right = sigmoid(proj[3 * hidden :]) * proj[2 * hidden : 3 * hidden]
    for half in range(wide.shape[0]):
        cols = slice(half * 128, half * 128 + 128)
        wide[half, pl.ds(r, hidden, stride=2 * rows), :] = left[:, cols]
        wide[half, pl.ds(rows + r, hidden, stride=2 * rows), :] = right[:, cols]


def pack(wide, out_ref):
    hidden, depth, _ = out_ref.shape

    def step(c, _):
        for half in range(wide.shape[0]):
            rows = wide[half, pl.ds(pl.multiple_of(c * 8 * depth, 8 * depth), 8 * depth), :]
            out_ref[pl.ds(c * 8, 8), :, half * 128 : half * 128 + 128] = rows.reshape(
                8, depth, 128
            ).astype(BF16)
        return 0

    lax.fori_loop(0, hidden // 8, step, 0)


def first_kernel(pair_ref, w_in_ref, out_ref, wide, w_t):
    rows, _, hidden = pair_ref.shape
    w_t[...] = turned(w_in_ref[...])

    def step(r, _):
        x = norm(pair_ref[r].astype(F32).T).astype(BF16)
        project(x, w_t[...], r, rows, wide, hidden)
        return 0

    lax.fori_loop(0, rows, step, 0, unroll=2)
    pack(wide, out_ref)


def first(pair, w_in):
    rows, cols, hidden = pair.shape
    return pl.pallas_call(
        first_kernel,
        out_shape=jax.ShapeDtypeStruct((hidden, 2 * rows, cols), BF16),
        in_specs=[VMEM, VMEM],
        out_specs=VMEM,
        scratch_shapes=[
            pltpu.VMEM((cols // 128, hidden * 2 * rows, 128), F32),
            pltpu.VMEM((w_in.shape[1], hidden), BF16),
        ],
        compiler_params=params(),
        name="first",
    )(pair, w_in)


def gate_kernel(pair_ref, w_gate_ref, z_ref, gate_ref, w_t):
    rows = pair_ref.shape[0]
    w_t[...] = turned(w_gate_ref[...])

    def step(r, _):
        z = pair_ref[r].astype(F32).T
        x = norm(z).astype(BF16)
        z_ref[r] = z.astype(BF16)
        gate_ref[r] = sigmoid(dot(w_t[...], x))
        return 0

    lax.fori_loop(0, rows, step, 0, unroll=2)


def gate(pair, w_gate):
    rows, cols, hidden = pair.shape
    return pl.pallas_call(
        gate_kernel,
        out_shape=(
            jax.ShapeDtypeStruct((rows, hidden, cols), BF16),
            jax.ShapeDtypeStruct((rows, hidden, cols), F32),
        ),
        in_specs=[VMEM, VMEM],
        out_specs=(VMEM, VMEM),
        scratch_shapes=[pltpu.VMEM((hidden, hidden), BF16)],
        compiler_params=params(),
        name="gate",
    )(pair, w_gate)


def gate_turned_kernel(z_ref, w_gate_ref, gate_ref, w_t):
    w_t[...] = turned(w_gate_ref[...])

    def step(r, _):
        x = norm(z_ref[r].astype(F32)).astype(BF16)
        gate_ref[r] = sigmoid(dot(w_t[...], x))
        return 0

    lax.fori_loop(0, z_ref.shape[0], step, 0, unroll=2)


def gate_turned(z, w_gate):
    rows, hidden, cols = z.shape
    return pl.pallas_call(
        gate_turned_kernel,
        out_shape=jax.ShapeDtypeStruct((rows, hidden, cols), F32),
        in_specs=[VMEM, VMEM],
        out_specs=VMEM,
        scratch_shapes=[pltpu.VMEM((hidden, hidden), BF16)],
        compiler_params=params(),
        name="gate_turned",
    )(z, w_gate)


def outgoing_kernel(add, which_ref, got_ref, *refs):
    out_ref = refs[-1]
    blocks, _, depth, cols = got_ref.shape
    rows = depth // 2
    per = cols // rows
    for yo in range(2):
        at = (yo * 2 + which_ref[0]) * per
        total = None
        for yk in range(2):
            a = got_ref[:, yk, :rows, :].reshape(blocks * rows, cols)
            b = got_ref[pl.ds(at, per), yk, rows:, :].reshape(cols, cols)
            part = lax.dot_general(a, b, (((1,), (1,)), ((), ())), preferred_element_type=F32)
            total = part if total is None else total + part
        total = total.reshape(blocks, rows, cols)
        if add:
            total = total + refs[0][:, yo].astype(F32)
        out_ref[:, yo] = total.astype(BF16)


def outgoing(got, core):
    src, depth, cols = got.shape
    got = got.reshape(src // 2, 2, depth, cols)
    shape = jax.ShapeDtypeStruct((src // 2, 2, depth // 2, cols), BF16)

    def call(add, which, *more):
        return pl.pallas_call(
            functools.partial(outgoing_kernel, add),
            out_shape=shape,
            in_specs=[SMEM, VMEM] + [VMEM] * len(more),
            out_specs=VMEM,
            compiler_params=params(),
            name="outgoing",
        )(which, got, *more)

    other = call(False, (1 - core).reshape(1))
    other = lax.ppermute(other, "core", [(0, 1), (1, 0)])
    return call(True, core.reshape(1), other).reshape(src, depth // 2, cols)


def incoming_kernel(which_ref, got_ref, left_ref, out_ref):
    blocks, _, depth, cols = got_ref.shape
    rows = depth // 2
    per = cols // rows
    for own in (True, False):
        core = which_ref[0] if own else 1 - which_ref[0]
        for yi in range(2):
            left = got_ref[:, yi, :rows, :] if own else left_ref[:, yi]
            left = left.reshape(blocks * rows, cols)
            at = (yi * 2 + core) * per
            for yo in range(2):
                right = got_ref[:, yo, rows:, :].reshape(blocks * rows, cols)
                part = lax.dot_general(
                    left, right, (((0,), (0,)), ((), ())), preferred_element_type=F32
                )
                out_ref[pl.ds(at, per), yo] = part.reshape(per, rows, cols).astype(BF16)


def incoming(got, core):
    src, depth, cols = got.shape
    got = got.reshape(src // 2, 2, depth, cols)
    left = lax.ppermute(got[:, :, : depth // 2], "core", [(0, 1), (1, 0)])
    out = pl.pallas_call(
        incoming_kernel,
        out_shape=jax.ShapeDtypeStruct((src // 2, 2, depth // 2, cols), BF16),
        in_specs=[SMEM, VMEM, VMEM],
        out_specs=VMEM,
        compiler_params=params(),
        name="incoming",
    )(core.reshape(1), got, left)
    return out.reshape(src, depth // 2, cols)


def normed_rows(tri_ref, flat):
    hidden, rows, cols = tri_ref.shape
    for half in range(cols // 128):
        lanes = slice(half * 128, half * 128 + 128)
        zero = jnp.zeros((rows, 128), F32)

        def add(c, total):
            return total + tri_ref[c, :, lanes].astype(F32)

        mean = lax.fori_loop(0, hidden, add, zero, unroll=8) * (1.0 / hidden)

        def square(c, total):
            centred = tri_ref[c, :, lanes].astype(F32) - mean
            return total + centred * centred

        var = lax.fori_loop(0, hidden, square, zero, unroll=8) * (1.0 / hidden)
        scale = lax.rsqrt(var + 1e-05)

        def write(c, _):
            flat[half, pl.ds(pl.multiple_of(c * rows, rows), rows), :] = (
                tri_ref[c, :, lanes].astype(F32) - mean
            ) * scale
            return 0

        lax.fori_loop(0, hidden, write, 0, unroll=8)


def row_of(flat, r, hidden, rows):
    return jnp.concatenate(
        [flat[half, pl.ds(r, hidden, stride=rows), :] for half in range(flat.shape[0])], axis=1
    ).astype(BF16)


def middle_kernel(tri_ref, z_ref, gate_ref, w_out_ref, w_in_ref, out_ref, z_new_ref, flat, wide, w_out_t, w_in_t):
    hidden, rows, _ = tri_ref.shape
    w_out_t[...] = turned(w_out_ref[...])
    w_in_t[...] = turned(w_in_ref[...])
    normed_rows(tri_ref, flat)

    def step(r, _):
        update = gate_ref[r] * dot(w_out_t[...], row_of(flat, r, hidden, rows))
        z = (z_ref[r].astype(F32) + update).astype(BF16)
        z_new_ref[r] = z
        x = norm(z.astype(F32)).astype(BF16)
        project(x, w_in_t[...], r, rows, wide, hidden)
        return 0

    lax.fori_loop(0, rows, step, 0, unroll=2)
    pack(wide, out_ref)


def middle(tri, z, gates, w_out, w_in):
    hidden, rows, cols = tri.shape
    return pl.pallas_call(
        middle_kernel,
        out_shape=(
            jax.ShapeDtypeStruct((hidden, 2 * rows, cols), BF16),
            jax.ShapeDtypeStruct((rows, hidden, cols), BF16),
        ),
        in_specs=[VMEM] * 5,
        out_specs=(VMEM, VMEM),
        scratch_shapes=[
            pltpu.VMEM((cols // 128, hidden * rows, 128), F32),
            pltpu.VMEM((cols // 128, hidden * 2 * rows, 128), F32),
            pltpu.VMEM((hidden, hidden), BF16),
            pltpu.VMEM((w_in.shape[1], hidden), BF16),
        ],
        compiler_params=params(),
        name="middle",
    )(tri, z, gates, w_out, w_in)


def last_kernel(tri_ref, z_ref, gate_ref, w_out_ref, out_ref, flat, w_out_t):
    hidden, rows, _ = tri_ref.shape
    w_out_t[...] = turned(w_out_ref[...])
    normed_rows(tri_ref, flat)

    def step(r, _):
        update = gate_ref[r] * dot(w_out_t[...], row_of(flat, r, hidden, rows))
        out_ref[r] = (z_ref[r].astype(F32) + update).T.astype(BF16)
        return 0

    lax.fori_loop(0, rows, step, 0, unroll=2)


def last(tri, z, gates, w_out):
    hidden, rows, cols = tri.shape
    return pl.pallas_call(
        last_kernel,
        out_shape=jax.ShapeDtypeStruct((rows, cols, hidden), BF16),
        in_specs=[VMEM] * 4,
        out_specs=VMEM,
        scratch_shapes=[
            pltpu.VMEM((cols // 128, hidden * rows, 128), F32),
            pltpu.VMEM((hidden, hidden), BF16),
        ],
        compiler_params=params(),
        name="last",
    )(tri, z, gates, w_out)


def exchange(blocks):
    return lax.all_to_all(blocks, CHIPS, split_axis=0, concat_axis=0, tiled=True)


def on_device(pair, w_in, w_gate, w_out):
    core = lax.axis_index("core")
    z, gates = gate(pair, w_gate[0])
    got = exchange(first(pair, w_in[0]))
    tri = exchange(outgoing(got, core))
    sent, z = middle(tri, z, gates, w_out[0], w_in[1])
    gates = gate_turned(z, w_gate[1])
    got = exchange(sent)
    tri = exchange(incoming(got, core))
    return last(tri, z, gates, w_out[1])


def solution(mesh):
    mesh = Mesh(mesh.devices.reshape(8, 4, 2, 2, 2), AXES)
    placed = P(("z", "x", "yl"), ("yh", "core"), None)
    return jax.shard_map(
        on_device, mesh=mesh, in_specs=(placed, P(), P(), P()), out_specs=placed, check_vma=False
    )
```

```python
import functools

import jax
import jax.numpy as jnp
from jax import lax
from jax.experimental import pallas as pl
from jax.experimental.pallas import tpu as pltpu
from jax.sharding import Mesh, PartitionSpec as P

AXES = ("z", "x", "yl", "yh", "core")
CHIPS = ("z", "x", "yl", "yh")
F32, BF16 = jnp.float32, jnp.bfloat16
VMEM = pl.BlockSpec(memory_space=pltpu.VMEM)
SMEM = pl.BlockSpec(memory_space=pltpu.SMEM)


def params():
    return pltpu.CompilerParams(vmem_limit_bytes=24 * 1024 * 1024)


def sigmoid(v):
    return 0.5 * jnp.tanh(0.5 * v) + 0.5


def norm(v):
    mean = jnp.mean(v, axis=0, keepdims=True)
    centred = v - mean
    var = jnp.mean(centred * centred, axis=0, keepdims=True)
    return centred * lax.rsqrt(var + 1e-05)


def turned(w):
    return w.astype(F32).T.astype(BF16)


def dot(a, b):
    return jnp.dot(a, b, preferred_element_type=F32)


def project(x, w_t, r, sides, hidden):
    proj = dot(w_t, x)
    for side in range(2):
        at = 2 * side * hidden
        gates = sigmoid(proj[at + hidden : at + 2 * hidden])
        sides[side, r] = (gates * proj[at : at + hidden]).astype(BF16)


def by_channel(sides, out_ref):
    _, rows, hidden, cols = sides.shape
    for side in range(2):
        for lane in range(0, cols, 128):
            for c in range(0, hidden, 32):
                block = sides[side, :, c : c + 32, lane : lane + 128]
                out_ref[c : c + 32, side * rows : side * rows + rows, lane : lane + 128] = (
                    jnp.swapaxes(block, 0, 1)
                )


def by_row(tri_ref, tri):
    hidden, _, cols = tri_ref.shape
    for lane in range(0, cols, 128):
        for c in range(0, hidden, 32):
            block = tri_ref[c : c + 32, :, lane : lane + 128]
            tri[:, c : c + 32, lane : lane + 128] = jnp.swapaxes(block, 0, 1)


def first_kernel(pair_ref, w_in_ref, out_ref, sides, w_t):
    rows, _, hidden = pair_ref.shape
    w_t[...] = turned(w_in_ref[0])
    for r in range(rows):
        x = norm(pair_ref[r].astype(F32).T).astype(BF16)
        project(x, w_t[...], r, sides, hidden)
    by_channel(sides, out_ref)


def first(pair, w_in):
    rows, cols, hidden = pair.shape
    return pl.pallas_call(
        first_kernel,
        out_shape=jax.ShapeDtypeStruct((hidden, 2 * rows, cols), BF16),
        in_specs=[VMEM, VMEM],
        out_specs=VMEM,
        scratch_shapes=[
            pltpu.VMEM((2, rows, hidden, cols), BF16),
            pltpu.VMEM((w_in.shape[2], hidden), BF16),
        ],
        compiler_params=params(),
        name="first",
    )(pair, w_in)


def gate_kernel(pair_ref, w_gate_ref, z_ref, gate_ref, w_t):
    w_t[...] = turned(w_gate_ref[0])
    for r in range(pair_ref.shape[0]):
        z = pair_ref[r].astype(F32).T
        z_ref[r] = z.astype(BF16)
        gate_ref[r] = sigmoid(dot(w_t[...], norm(z).astype(BF16)))


def gate(pair, w_gate):
    rows, cols, hidden = pair.shape
    return pl.pallas_call(
        gate_kernel,
        out_shape=(
            jax.ShapeDtypeStruct((rows, hidden, cols), BF16),
            jax.ShapeDtypeStruct((rows, hidden, cols), F32),
        ),
        in_specs=[VMEM, VMEM],
        out_specs=(VMEM, VMEM),
        scratch_shapes=[pltpu.VMEM((hidden, hidden), BF16)],
        compiler_params=params(),
        name="gate",
    )(pair, w_gate)


def gate_turned_kernel(z_ref, w_gate_ref, gate_ref, w_t):
    w_t[...] = turned(w_gate_ref[1])
    for r in range(z_ref.shape[0]):
        gate_ref[r] = sigmoid(dot(w_t[...], norm(z_ref[r].astype(F32)).astype(BF16)))


def gate_turned(z, w_gate):
    rows, hidden, cols = z.shape
    return pl.pallas_call(
        gate_turned_kernel,
        out_shape=jax.ShapeDtypeStruct((rows, hidden, cols), F32),
        in_specs=[VMEM, VMEM],
        out_specs=VMEM,
        scratch_shapes=[pltpu.VMEM((hidden, hidden), BF16)],
        compiler_params=params(),
        name="gate_turned",
    )(z, w_gate)


def outgoing_kernel(add, which_ref, got_ref, *refs):
    out_ref = refs[-1]
    blocks, _, depth, cols = got_ref.shape
    rows = depth // 2
    per = cols // rows
    for yo in range(2):
        at = (yo * 2 + which_ref[0]) * per
        total = None
        for yk in range(2):
            a = got_ref[:, yk, :rows, :].reshape(blocks * rows, cols)
            b = got_ref[pl.ds(at, per), yk, rows:, :].reshape(cols, cols)
            part = lax.dot_general(a, b, (((1,), (1,)), ((), ())), preferred_element_type=F32)
            total = part if total is None else total + part
        total = total.reshape(blocks, rows, cols)
        if add:
            total = total + refs[0][:, yo].astype(F32)
        out_ref[:, yo] = total.astype(BF16)


def outgoing(got, core):
    src, depth, cols = got.shape
    got = got.reshape(src // 2, 2, depth, cols)
    shape = jax.ShapeDtypeStruct((src // 2, 2, depth // 2, cols), BF16)

    def call(add, which, *more):
        return pl.pallas_call(
            functools.partial(outgoing_kernel, add),
            out_shape=shape,
            in_specs=[SMEM, VMEM] + [VMEM] * len(more),
            out_specs=VMEM,
            compiler_params=params(),
            name="outgoing",
        )(which, got, *more)

    other = call(False, (1 - core).reshape(1))
    other = lax.ppermute(other, "core", [(0, 1), (1, 0)])
    return call(True, core.reshape(1), other).reshape(src, depth // 2, cols)


def incoming_kernel(which_ref, got_ref, left_ref, out_ref):
    blocks, _, depth, cols = got_ref.shape
    rows = depth // 2
    per = cols // rows
    for own in (True, False):
        core = which_ref[0] if own else 1 - which_ref[0]
        for yi in range(2):
            left = got_ref[:, yi, :rows, :] if own else left_ref[:, yi]
            left = left.reshape(blocks * rows, cols)
            at = (yi * 2 + core) * per
            for yo in range(2):
                right = got_ref[:, yo, rows:, :].reshape(blocks * rows, cols)
                part = lax.dot_general(
                    left, right, (((0,), (0,)), ((), ())), preferred_element_type=F32
                )
                out_ref[pl.ds(at, per), yo] = part.reshape(per, rows, cols).astype(BF16)


def incoming(got, core):
    src, depth, cols = got.shape
    got = got.reshape(src // 2, 2, depth, cols)
    left = lax.ppermute(got[:, :, : depth // 2], "core", [(0, 1), (1, 0)])
    out = pl.pallas_call(
        incoming_kernel,
        out_shape=jax.ShapeDtypeStruct((src // 2, 2, depth // 2, cols), BF16),
        in_specs=[SMEM, VMEM, VMEM],
        out_specs=VMEM,
        compiler_params=params(),
        name="incoming",
    )(core.reshape(1), got, left)
    return out.reshape(src, depth // 2, cols)


def updated(tri, z_ref, gate_ref, w_out_t, r):
    y = norm(tri[r].astype(F32)).astype(BF16)
    return z_ref[r].astype(F32) + gate_ref[r] * dot(w_out_t[...], y)


def middle_kernel(
    tri_ref, z_ref, gate_ref, w_out_ref, w_in_ref, out_ref, z_new_ref, tri, sides, w_out_t, w_in_t
):
    hidden, rows, _ = tri_ref.shape
    w_out_t[...] = turned(w_out_ref[0])
    w_in_t[...] = turned(w_in_ref[1])
    by_row(tri_ref, tri)
    for r in range(rows):
        z = updated(tri, z_ref, gate_ref, w_out_t, r).astype(BF16)
        z_new_ref[r] = z
        project(norm(z.astype(F32)).astype(BF16), w_in_t[...], r, sides, hidden)
    by_channel(sides, out_ref)


def middle(tri, z, gates, w_out, w_in):
    hidden, rows, cols = tri.shape
    return pl.pallas_call(
        middle_kernel,
        out_shape=(
            jax.ShapeDtypeStruct((hidden, 2 * rows, cols), BF16),
            jax.ShapeDtypeStruct((rows, hidden, cols), BF16),
        ),
        in_specs=[VMEM] * 5,
        out_specs=(VMEM, VMEM),
        scratch_shapes=[
            pltpu.VMEM((rows, hidden, cols), BF16),
            pltpu.VMEM((2, rows, hidden, cols), BF16),
            pltpu.VMEM((hidden, hidden), BF16),
            pltpu.VMEM((w_in.shape[2], hidden), BF16),
        ],
        compiler_params=params(),
        name="middle",
    )(tri, z, gates, w_out, w_in)


def last_kernel(tri_ref, z_ref, gate_ref, w_out_ref, out_ref, tri, w_out_t):
    w_out_t[...] = turned(w_out_ref[1])
    by_row(tri_ref, tri)
    for r in range(tri_ref.shape[1]):
        out_ref[r] = updated(tri, z_ref, gate_ref, w_out_t, r).T.astype(BF16)


def last(tri, z, gates, w_out):
    hidden, rows, cols = tri.shape
    return pl.pallas_call(
        last_kernel,
        out_shape=jax.ShapeDtypeStruct((rows, cols, hidden), BF16),
        in_specs=[VMEM] * 4,
        out_specs=VMEM,
        scratch_shapes=[
            pltpu.VMEM((rows, hidden, cols), BF16),
            pltpu.VMEM((hidden, hidden), BF16),
        ],
        compiler_params=params(),
        name="last",
    )(tri, z, gates, w_out)


def exchange(blocks):
    return lax.all_to_all(blocks, CHIPS, split_axis=0, concat_axis=0, tiled=True)


def on_device(pair, w_in, w_gate, w_out):
    core = lax.axis_index("core")
    z, gates = gate(pair, w_gate)
    got = exchange(first(pair, w_in))
    tri = exchange(outgoing(got, core))
    sent, z = middle(tri, z, gates, w_out, w_in)
    gates = gate_turned(z, w_gate)
    got = exchange(sent)
    tri = exchange(incoming(got, core))
    return last(tri, z, gates, w_out)


def solution(mesh):
    mesh = Mesh(mesh.devices.reshape(8, 4, 2, 2, 2), AXES)
    placed = P(("z", "x", "yl"), ("yh", "core"), None)
    return jax.shard_map(
        on_device, mesh=mesh, in_specs=(placed, P(), P(), P()), out_specs=placed, check_vma=False
    )
```

```python
import jax
import jax.numpy as jnp
from jax import lax
from jax.experimental import pallas as pl
from jax.experimental.pallas import tpu as pltpu
from jax.sharding import Mesh, PartitionSpec as P

AXES = ("z", "x", "yl", "yh", "core")
CHIPS = ("z", "x", "yl", "yh")
F32, BF16 = jnp.float32, jnp.bfloat16
VMEM = pl.BlockSpec(memory_space=pltpu.VMEM)
SMEM = pl.BlockSpec(memory_space=pltpu.SMEM)
HBM = pl.BlockSpec(memory_space=pltpu.HBM)


def params():
    return pltpu.CompilerParams(vmem_limit_bytes=24 * 1024 * 1024)


def sigmoid(v):
    return 0.5 * jnp.tanh(0.5 * v) + 0.5


def norm(v):
    mean = jnp.mean(v, axis=0, keepdims=True)
    centred = v - mean
    var = jnp.mean(centred * centred, axis=0, keepdims=True)
    return centred * lax.rsqrt(var + 1e-05)


def turned(w):
    return w.astype(F32).T.astype(BF16)


def dot(a, b):
    return jnp.dot(a, b, preferred_element_type=F32)


def project(x, w_t, r, sides, hidden):
    proj = dot(w_t, x)
    for side in range(2):
        at = 2 * side * hidden
        gates = sigmoid(proj[at + hidden : at + 2 * hidden])
        sides[side, r] = (gates * proj[at : at + hidden]).astype(BF16)


def by_channel(sides, out_ref):
    _, rows, hidden, cols = sides.shape
    for side in range(2):
        for lane in range(0, cols, 128):
            for c in range(0, hidden, 32):
                block = sides[side, :, c : c + 32, lane : lane + 128]
                out_ref[c : c + 32, side * rows : side * rows + rows, lane : lane + 128] = (
                    jnp.swapaxes(block, 0, 1)
                )


def by_row(tri_ref, tri):
    hidden, _, cols = tri_ref.shape
    for lane in range(0, cols, 128):
        for c in range(0, hidden, 32):
            block = tri_ref[c : c + 32, :, lane : lane + 128]
            tri[:, c : c + 32, lane : lane + 128] = jnp.swapaxes(block, 0, 1)


def first_kernel(pair_ref, w_in_ref, out_ref, sides, w_t):
    rows, _, hidden = pair_ref.shape
    w_t[...] = turned(w_in_ref[0])
    for r in range(rows):
        x = norm(pair_ref[r].astype(F32).T).astype(BF16)
        project(x, w_t[...], r, sides, hidden)
    by_channel(sides, out_ref)


def first(pair, w_in):
    rows, cols, hidden = pair.shape
    return pl.pallas_call(
        first_kernel,
        out_shape=jax.ShapeDtypeStruct((hidden, 2 * rows, cols), BF16),
        in_specs=[VMEM, VMEM],
        out_specs=VMEM,
        scratch_shapes=[
            pltpu.VMEM((2, rows, hidden, cols), BF16),
            pltpu.VMEM((w_in.shape[2], hidden), BF16),
        ],
        compiler_params=params(),
        name="first",
    )(pair, w_in)


def products(got_ref, yo, core):
    blocks, _, depth, cols = got_ref.shape
    rows = depth // 2
    per = cols // rows
    total = None
    for yk in range(2):
        a = got_ref[:, yk, :rows, :].reshape(blocks * rows, cols)
        b = got_ref[pl.ds((yo * 2 + core) * per, per), yk, rows:, :].reshape(cols, cols)
        part = lax.dot_general(a, b, (((1,), (1,)), ((), ())), preferred_element_type=F32)
        total = part if total is None else total + part
    return total.reshape(blocks, rows, cols)


def other_kernel(core_ref, got_ref, out_ref):
    for yo in range(2):
        out_ref[:, yo] = products(got_ref, yo, 1 - core_ref[0]).astype(BF16)


def own_kernel(core_ref, got_ref, pair_ref, w_gate_ref, own_ref, z_ref, gate_ref, w_t):
    for yo in range(2):
        own_ref[:, yo] = products(got_ref, yo, core_ref[0])
    w_t[...] = turned(w_gate_ref[0])
    for r in range(pair_ref.shape[0]):
        z = pair_ref[r].astype(F32).T
        z_ref[r] = z.astype(BF16)
        gate_ref[r] = sigmoid(dot(w_t[...], norm(z).astype(BF16)))


def sum_kernel(own_ref, other_ref, out_ref):
    out_ref[...] = (own_ref[...] + other_ref[...].astype(F32)).astype(BF16)


def outgoing(got, core, pair, w_gate):
    src, depth, cols = got.shape
    rows, _, hidden = pair.shape
    got = got.reshape(src // 2, 2, depth, cols)
    tri = (src // 2, 2, depth // 2, cols)
    other = pl.pallas_call(
        other_kernel,
        out_shape=jax.ShapeDtypeStruct(tri, BF16),
        in_specs=[SMEM, VMEM],
        out_specs=VMEM,
        compiler_params=params(),
        name="other",
    )(core, got)
    other = lax.ppermute(other, "core", [(0, 1), (1, 0)])
    own, z, gates = pl.pallas_call(
        own_kernel,
        out_shape=(
            jax.ShapeDtypeStruct(tri, F32),
            jax.ShapeDtypeStruct((rows, hidden, cols), BF16),
            jax.ShapeDtypeStruct((rows, hidden, cols), F32),
        ),
        in_specs=[SMEM, VMEM, VMEM, VMEM],
        out_specs=(VMEM,) * 3,
        scratch_shapes=[pltpu.VMEM((hidden, hidden), BF16)],
        compiler_params=params(),
        name="own",
    )(core, got, pair, w_gate)
    summed = pl.pallas_call(
        sum_kernel,
        out_shape=jax.ShapeDtypeStruct(tri, BF16),
        in_specs=[VMEM, VMEM],
        out_specs=VMEM,
        compiler_params=params(),
        name="sum",
    )(own, other)
    return summed.reshape(src, depth // 2, cols), z, gates


def columns(left, got_ref, yo):
    blocks, _, depth, cols = got_ref.shape
    rows = depth // 2
    right = got_ref[:, yo, rows:, :].reshape(blocks * rows, cols)
    part = lax.dot_general(
        left.reshape(blocks * rows, cols),
        right,
        (((0,), (0,)), ((), ())),
        preferred_element_type=F32,
    )
    return part.reshape(cols // rows, rows, cols).astype(BF16)


def near_kernel(got_ref, z_ref, w_gate_ref, near_ref, gate_ref, w_t):
    rows = z_ref.shape[0]
    per = near_ref.shape[0] // 2
    for yi in range(2):
        for yo in range(2):
            near_ref[yi * per : yi * per + per, yo] = columns(got_ref[:, yi, :rows, :], got_ref, yo)
    w_t[...] = turned(w_gate_ref[1])
    for r in range(rows):
        gate_ref[r] = sigmoid(dot(w_t[...], norm(z_ref[r].astype(F32)).astype(BF16)))


def far_kernel(core_ref, got_ref, left_ref, near_ref, out_ref):
    per = near_ref.shape[0] // 2
    core = core_ref[0]
    for yi in range(2):
        out_ref[pl.ds((yi * 2 + core) * per, per)] = near_ref[yi * per : yi * per + per]
        for yo in range(2):
            out_ref[pl.ds((yi * 2 + 1 - core) * per, per), yo] = columns(left_ref[:, yi], got_ref, yo)


def incoming(got, core, z, w_gate):
    src, depth, cols = got.shape
    rows, hidden, _ = z.shape
    got = got.reshape(src // 2, 2, depth, cols)
    left = lax.ppermute(got[:, :, : depth // 2], "core", [(0, 1), (1, 0)])
    near, gates = pl.pallas_call(
        near_kernel,
        out_shape=(
            jax.ShapeDtypeStruct((2 * cols // rows, 2, rows, cols), BF16),
            jax.ShapeDtypeStruct((rows, hidden, cols), F32),
        ),
        in_specs=[VMEM, VMEM, VMEM],
        out_specs=(VMEM, VMEM),
        scratch_shapes=[pltpu.VMEM((hidden, hidden), BF16)],
        compiler_params=params(),
        name="near",
    )(got, z, w_gate)
    out = pl.pallas_call(
        far_kernel,
        out_shape=jax.ShapeDtypeStruct((src // 2, 2, depth // 2, cols), BF16),
        in_specs=[SMEM, VMEM, VMEM, VMEM],
        out_specs=VMEM,
        compiler_params=params(),
        name="far",
    )(core, got, left, near)
    return out.reshape(src, depth // 2, cols), gates


def updated(tri, z_ref, gate_ref, w_out_t, r):
    y = norm(tri[r].astype(F32)).astype(BF16)
    return z_ref[r].astype(F32) + gate_ref[r] * dot(w_out_t[...], y)


def middle_kernel(
    tri_ref, z_ref, gate_ref, w_out_ref, w_in_ref, out_ref, z_new_ref, tri, sides, w_out_t, w_in_t
):
    hidden, rows, _ = tri_ref.shape
    w_out_t[...] = turned(w_out_ref[0])
    w_in_t[...] = turned(w_in_ref[1])
    by_row(tri_ref, tri)
    for r in range(rows):
        z = updated(tri, z_ref, gate_ref, w_out_t, r).astype(BF16)
        z_new_ref[r] = z
        project(norm(z.astype(F32)).astype(BF16), w_in_t[...], r, sides, hidden)
    by_channel(sides, out_ref)


def middle(tri, z, gates, w_out, w_in):
    hidden, rows, cols = tri.shape
    return pl.pallas_call(
        middle_kernel,
        out_shape=(
            jax.ShapeDtypeStruct((hidden, 2 * rows, cols), BF16),
            jax.ShapeDtypeStruct((rows, hidden, cols), BF16),
        ),
        in_specs=[VMEM] * 5,
        out_specs=(VMEM, VMEM),
        scratch_shapes=[
            pltpu.VMEM((rows, hidden, cols), BF16),
            pltpu.VMEM((2, rows, hidden, cols), BF16),
            pltpu.VMEM((hidden, hidden), BF16),
            pltpu.VMEM((w_in.shape[2], hidden), BF16),
        ],
        compiler_params=params(),
        name="middle",
    )(tri, z, gates, w_out, w_in)


def last_kernel(tri_ref, z_ref, gate_ref, w_out_ref, out_ref, tri, rows_out, w_out_t, sems):
    w_out_t[...] = turned(w_out_ref[1])
    by_row(tri_ref, tri)
    copies = []
    for r in range(tri_ref.shape[1]):
        rows_out[r] = updated(tri, z_ref, gate_ref, w_out_t, r).T.astype(BF16)
        copies.append(pltpu.make_async_copy(rows_out.at[r], out_ref.at[r], sems.at[r]))
        copies[-1].start()
    for copy in copies:
        copy.wait()


def last(tri, z, gates, w_out):
    hidden, rows, cols = tri.shape
    return pl.pallas_call(
        last_kernel,
        out_shape=jax.ShapeDtypeStruct((rows, cols, hidden), BF16),
        in_specs=[VMEM] * 4,
        out_specs=HBM,
        scratch_shapes=[
            pltpu.VMEM((rows, hidden, cols), BF16),
            pltpu.VMEM((rows, cols, hidden), BF16),
            pltpu.VMEM((hidden, hidden), BF16),
            pltpu.SemaphoreType.DMA((rows,)),
        ],
        compiler_params=params(),
        name="last",
    )(tri, z, gates, w_out)


def exchange(blocks):
    return lax.all_to_all(blocks, CHIPS, split_axis=0, concat_axis=0, tiled=True)


def on_device(pair, w_in, w_gate, w_out):
    core = lax.axis_index("core").reshape(1)
    got = exchange(first(pair, w_in))
    tri, z, gates = outgoing(got, core, pair, w_gate)
    sent, z = middle(exchange(tri), z, gates, w_out, w_in)
    tri, gates = incoming(exchange(sent), core, z, w_gate)
    return last(exchange(tri), z, gates, w_out)


def solution(mesh):
    mesh = Mesh(mesh.devices.reshape(8, 4, 2, 2, 2), AXES)
    placed = P(("z", "x", "yl"), ("yh", "core"), None)
    return jax.shard_map(
        on_device, mesh=mesh, in_specs=(placed, P(), P(), P()), out_specs=placed, check_vma=False
    )
```

```python
import jax
import jax.numpy as jnp
from jax import lax
from jax.experimental import pallas as pl
from jax.experimental.pallas import tpu as pltpu
from jax.sharding import Mesh, PartitionSpec as P

AXES = ("z", "x", "yl", "yh", "core")
CHIPS = ("z", "x", "yl", "yh")
F32, BF16 = jnp.float32, jnp.bfloat16
VMEM = pl.BlockSpec(memory_space=pltpu.VMEM)
SMEM = pl.BlockSpec(memory_space=pltpu.SMEM)
HBM = pl.BlockSpec(memory_space=pltpu.HBM)


def params():
    return pltpu.CompilerParams(vmem_limit_bytes=24 * 1024 * 1024)


def sigmoid(v):
    return 0.5 * jnp.tanh(0.5 * v) + 0.5


def norm(v):
    mean = jnp.mean(v, axis=0, keepdims=True)
    centred = v - mean
    var = jnp.mean(centred * centred, axis=0, keepdims=True)
    return centred * lax.rsqrt(var + 1e-05)


def turned(w):
    return w.astype(F32).T.astype(BF16)


def dot(a, b):
    return jnp.dot(a, b, preferred_element_type=F32)


def project(x, w_t, r, sides, hidden):
    proj = dot(w_t, x)
    for side in range(2):
        at = 2 * side * hidden
        gates = sigmoid(proj[at + hidden : at + 2 * hidden])
        sides[side, r] = (gates * proj[at : at + hidden]).astype(BF16)


def by_channel(sides, out_ref):
    _, rows, hidden, cols = sides.shape
    for side in range(2):
        for lane in range(0, cols, 128):
            for c in range(0, hidden, 32):
                block = sides[side, :, c : c + 32, lane : lane + 128]
                out_ref[c : c + 32, side * rows : side * rows + rows, lane : lane + 128] = (
                    jnp.swapaxes(block, 0, 1)
                )


def by_row(tri_ref, tri):
    hidden, _, cols = tri_ref.shape
    for lane in range(0, cols, 128):
        for c in range(0, hidden, 32):
            block = tri_ref[c : c + 32, :, lane : lane + 128]
            tri[:, c : c + 32, lane : lane + 128] = jnp.swapaxes(block, 0, 1)


def first_kernel(core_ref, pair_ref, w_in_ref, out_ref, z_ref, sides, w_t):
    rows, _, hidden = pair_ref.shape
    w_t[...] = turned(w_in_ref[0])
    for r in range(rows):
        z = pair_ref[r].astype(F32).T
        z_ref[r] = z.astype(BF16)
        project(norm(z).astype(BF16), w_t[...], r, sides, hidden)
    by_channel(sides, out_ref)


def first(core, pair, w_in):
    rows, cols, hidden = pair.shape
    return pl.pallas_call(
        first_kernel,
        out_shape=(
            jax.ShapeDtypeStruct((hidden, 2 * rows, cols), BF16),
            jax.ShapeDtypeStruct((rows, hidden, cols), BF16),
        ),
        in_specs=[SMEM, VMEM, VMEM],
        out_specs=(VMEM, VMEM),
        scratch_shapes=[
            pltpu.VMEM((2, rows, hidden, cols), BF16),
            pltpu.VMEM((w_in.shape[2], hidden), BF16),
        ],
        compiler_params=params(),
        name="first",
    )(core, pair, w_in)


def products(got_ref, yo, core):
    blocks, _, depth, cols = got_ref.shape
    rows = depth // 2
    per = cols // rows
    total = None
    for yk in range(2):
        a = got_ref[:, yk, :rows, :].reshape(blocks * rows, cols)
        b = got_ref[pl.ds((yo * 2 + core) * per, per), yk, rows:, :].reshape(cols, cols)
        part = lax.dot_general(a, b, (((1,), (1,)), ((), ())), preferred_element_type=F32)
        total = part if total is None else total + part
    return total.reshape(blocks, rows, cols)


def other_kernel(core_ref, got_ref, out_ref):
    for yo in range(2):
        out_ref[:, yo] = products(got_ref, yo, 1 - core_ref[0]).astype(BF16)


def own_kernel(core_ref, got_ref, z_ref, w_gate_ref, own_ref, gate_ref, w_t):
    for yo in range(2):
        own_ref[:, yo] = products(got_ref, yo, core_ref[0])
    w_t[...] = turned(w_gate_ref[0])
    for r in range(z_ref.shape[0]):
        gate_ref[r] = sigmoid(dot(w_t[...], norm(z_ref[r].astype(F32)).astype(BF16)))


def sum_kernel(own_ref, other_ref, out_ref):
    out_ref[...] = (own_ref[...] + other_ref[...].astype(F32)).astype(BF16)


def outgoing(got, core, z, w_gate):
    src, depth, cols = got.shape
    rows, hidden, _ = z.shape
    got = got.reshape(src // 2, 2, depth, cols)
    tri = (src // 2, 2, depth // 2, cols)
    other = pl.pallas_call(
        other_kernel,
        out_shape=jax.ShapeDtypeStruct(tri, BF16),
        in_specs=[SMEM, VMEM],
        out_specs=VMEM,
        compiler_params=params(),
        name="other",
    )(core, got)
    other = lax.ppermute(other, "core", [(0, 1), (1, 0)])
    own, gates = pl.pallas_call(
        own_kernel,
        out_shape=(
            jax.ShapeDtypeStruct(tri, F32),
            jax.ShapeDtypeStruct((rows, hidden, cols), F32),
        ),
        in_specs=[SMEM, VMEM, VMEM, VMEM],
        out_specs=(VMEM, VMEM),
        scratch_shapes=[pltpu.VMEM((hidden, hidden), BF16)],
        compiler_params=params(),
        name="own",
    )(core, got, z, w_gate)
    summed = pl.pallas_call(
        sum_kernel,
        out_shape=jax.ShapeDtypeStruct(tri, BF16),
        in_specs=[VMEM, VMEM],
        out_specs=VMEM,
        compiler_params=params(),
        name="sum",
    )(own, other)
    return summed.reshape(src, depth // 2, cols), gates


def columns(left, got_ref, yo):
    blocks, _, depth, cols = got_ref.shape
    rows = depth // 2
    right = got_ref[:, yo, rows:, :].reshape(blocks * rows, cols)
    part = lax.dot_general(
        left.reshape(blocks * rows, cols),
        right,
        (((0,), (0,)), ((), ())),
        preferred_element_type=F32,
    )
    return part.reshape(cols // rows, rows, cols).astype(BF16)


def near_kernel(got_ref, z_ref, w_gate_ref, near_ref, gate_ref, w_t):
    rows = z_ref.shape[0]
    per = near_ref.shape[0] // 2
    for yi in range(2):
        for yo in range(2):
            near_ref[yi * per : yi * per + per, yo] = columns(got_ref[:, yi, :rows, :], got_ref, yo)
    w_t[...] = turned(w_gate_ref[1])
    for r in range(rows):
        gate_ref[r] = sigmoid(dot(w_t[...], norm(z_ref[r].astype(F32)).astype(BF16)))


def far_kernel(core_ref, got_ref, left_ref, near_ref, out_ref):
    per = near_ref.shape[0] // 2
    core = core_ref[0]
    for yi in range(2):
        out_ref[pl.ds((yi * 2 + core) * per, per)] = near_ref[yi * per : yi * per + per]
        for yo in range(2):
            out_ref[pl.ds((yi * 2 + 1 - core) * per, per), yo] = columns(left_ref[:, yi], got_ref, yo)


def incoming(got, core, z, w_gate):
    src, depth, cols = got.shape
    rows, hidden, _ = z.shape
    got = got.reshape(src // 2, 2, depth, cols)
    left = lax.ppermute(got[:, :, : depth // 2], "core", [(0, 1), (1, 0)])
    near, gates = pl.pallas_call(
        near_kernel,
        out_shape=(
            jax.ShapeDtypeStruct((2 * cols // rows, 2, rows, cols), BF16),
            jax.ShapeDtypeStruct((rows, hidden, cols), F32),
        ),
        in_specs=[VMEM, VMEM, VMEM],
        out_specs=(VMEM, VMEM),
        scratch_shapes=[pltpu.VMEM((hidden, hidden), BF16)],
        compiler_params=params(),
        name="near",
    )(got, z, w_gate)
    out = pl.pallas_call(
        far_kernel,
        out_shape=jax.ShapeDtypeStruct((src // 2, 2, depth // 2, cols), BF16),
        in_specs=[SMEM, VMEM, VMEM, VMEM],
        out_specs=VMEM,
        compiler_params=params(),
        name="far",
    )(core, got, left, near)
    return out.reshape(src, depth // 2, cols), gates


def updated(tri, z_ref, gate_ref, w_out_t, r):
    y = norm(tri[r].astype(F32)).astype(BF16)
    return z_ref[r].astype(F32) + gate_ref[r] * dot(w_out_t[...], y)


def middle_kernel(
    tri_ref, z_ref, gate_ref, w_out_ref, w_in_ref, out_ref, z_new_ref, tri, sides, w_out_t, w_in_t
):
    hidden, rows, _ = tri_ref.shape
    w_out_t[...] = turned(w_out_ref[0])
    w_in_t[...] = turned(w_in_ref[1])
    by_row(tri_ref, tri)
    for r in range(rows):
        z = updated(tri, z_ref, gate_ref, w_out_t, r).astype(BF16)
        z_new_ref[r] = z
        project(norm(z.astype(F32)).astype(BF16), w_in_t[...], r, sides, hidden)
    by_channel(sides, out_ref)


def middle(tri, z, gates, w_out, w_in):
    hidden, rows, cols = tri.shape
    return pl.pallas_call(
        middle_kernel,
        out_shape=(
            jax.ShapeDtypeStruct((hidden, 2 * rows, cols), BF16),
            jax.ShapeDtypeStruct((rows, hidden, cols), BF16),
        ),
        in_specs=[VMEM] * 5,
        out_specs=(VMEM, VMEM),
        scratch_shapes=[
            pltpu.VMEM((rows, hidden, cols), BF16),
            pltpu.VMEM((2, rows, hidden, cols), BF16),
            pltpu.VMEM((hidden, hidden), BF16),
            pltpu.VMEM((w_in.shape[2], hidden), BF16),
        ],
        compiler_params=params(),
        name="middle",
    )(tri, z, gates, w_out, w_in)


def last_kernel(tri_ref, z_ref, gate_ref, w_out_ref, out_ref, tri, rows_out, w_out_t, sems):
    w_out_t[...] = turned(w_out_ref[1])
    by_row(tri_ref, tri)
    copies = []
    for r in range(tri_ref.shape[1]):
        rows_out[r] = updated(tri, z_ref, gate_ref, w_out_t, r).T.astype(BF16)
        copies.append(pltpu.make_async_copy(rows_out.at[r], out_ref.at[r], sems.at[r]))
        copies[-1].start()
    for copy in copies:
        copy.wait()


def last(tri, z, gates, w_out):
    hidden, rows, cols = tri.shape
    return pl.pallas_call(
        last_kernel,
        out_shape=jax.ShapeDtypeStruct((rows, cols, hidden), BF16),
        in_specs=[VMEM] * 4,
        out_specs=HBM,
        scratch_shapes=[
            pltpu.VMEM((rows, hidden, cols), BF16),
            pltpu.VMEM((rows, cols, hidden), BF16),
            pltpu.VMEM((hidden, hidden), BF16),
            pltpu.SemaphoreType.DMA((rows,)),
        ],
        compiler_params=params(),
        name="last",
    )(tri, z, gates, w_out)


def exchange(blocks):
    return lax.all_to_all(blocks, CHIPS, split_axis=0, concat_axis=0, tiled=True)


def on_device(pair, w_in, w_gate, w_out):
    core = lax.axis_index("core").reshape(1)
    sent, z = first(core, pair, w_in)
    tri, gates = outgoing(exchange(sent), core, z, w_gate)
    sent, z = middle(exchange(tri), z, gates, w_out, w_in)
    tri, gates = incoming(exchange(sent), core, z, w_gate)
    return last(exchange(tri), z, gates, w_out)


def solution(mesh):
    mesh = Mesh(mesh.devices.reshape(8, 4, 2, 2, 2), AXES)
    placed = P(("z", "x", "yl"), ("yh", "core"), None)
    return jax.shard_map(
        on_device, mesh=mesh, in_specs=(placed, P(), P(), P()), out_specs=placed, check_vma=False
    )
```

```python
import jax
import jax.numpy as jnp
from jax import lax
from jax.experimental import pallas as pl
from jax.experimental.pallas import tpu as pltpu
from jax.sharding import Mesh, PartitionSpec as P

AXES = ("z", "x", "yl", "yh", "core")
CHIPS = ("z", "x", "yl", "yh")
F32, BF16 = jnp.float32, jnp.bfloat16
VMEM = pl.BlockSpec(memory_space=pltpu.VMEM)
SMEM = pl.BlockSpec(memory_space=pltpu.SMEM)
HBM = pl.BlockSpec(memory_space=pltpu.HBM)


def params():
    return pltpu.CompilerParams(vmem_limit_bytes=14 * 1024 * 1024)


def sigmoid(v):
    return 0.5 * jnp.tanh(0.5 * v) + 0.5


def norm(v):
    mean = jnp.mean(v, axis=0, keepdims=True)
    centred = v - mean
    var = jnp.mean(centred * centred, axis=0, keepdims=True)
    return centred * lax.rsqrt(var + 1e-05)


def turned(w):
    return w.astype(F32).T.astype(BF16)


def dot(a, b):
    return jnp.dot(a, b, preferred_element_type=F32)


def project(x, w_t, r, sides, hidden):
    proj = dot(w_t, x)
    for side in range(2):
        at = 2 * side * hidden
        gates = sigmoid(proj[at + hidden : at + 2 * hidden])
        sides[side, r] = (gates * proj[at : at + hidden]).astype(BF16)


def by_channel(sides, out_ref):
    _, rows, hidden, cols = sides.shape
    for side in range(2):
        for lane in range(0, cols, 128):
            for c in range(0, hidden, 32):
                block = sides[side, :, c : c + 32, lane : lane + 128]
                out_ref[c : c + 32, side * rows : side * rows + rows, lane : lane + 128] = (
                    jnp.swapaxes(block, 0, 1)
                )


def by_row(tri_refs, tri):
    for at, tri_ref in enumerate(tri_refs):
        hidden, _, cols = tri_ref.shape
        for lane in range(0, cols, 128):
            for c in range(0, hidden, 32):
                block = tri_ref[c : c + 32, :, lane : lane + 128]
                tri[:, c : c + 32, at * cols + lane : at * cols + lane + 128] = jnp.swapaxes(block, 0, 1)


def first_kernel(core_ref, pair_ref, w_in_ref, out_ref, z_ref, sides, w_t):
    rows, _, hidden = pair_ref.shape
    w_t[...] = turned(w_in_ref[0])
    for r in range(rows):
        z = pair_ref[r].astype(F32).T
        z_ref[r] = z.astype(BF16)
        project(norm(z).astype(BF16), w_t[...], r, sides, hidden)
    by_channel(sides, out_ref)


def first(core, pair, w_in):
    rows, cols, hidden = pair.shape
    return pl.pallas_call(
        first_kernel,
        out_shape=(
            jax.ShapeDtypeStruct((hidden, 2 * rows, cols), BF16),
            jax.ShapeDtypeStruct((rows, hidden, cols), BF16),
        ),
        in_specs=[SMEM, VMEM, VMEM],
        out_specs=(VMEM, VMEM),
        scratch_shapes=[
            pltpu.VMEM((2, rows, hidden, cols), BF16),
            pltpu.VMEM((w_in.shape[2], hidden), BF16),
        ],
        compiler_params=params(),
        name="first",
    )(core, pair, w_in)


def products(got_ref, yo, core):
    blocks, _, depth, cols = got_ref.shape
    rows = depth // 2
    per = cols // rows
    total = None
    for yk in range(2):
        a = got_ref[:, yk, :rows, :].reshape(blocks * rows, cols)
        b = got_ref[pl.ds((yo * 2 + core) * per, per), yk, rows:, :].reshape(cols, cols)
        part = lax.dot_general(a, b, (((1,), (1,)), ((), ())), preferred_element_type=F32)
        total = part if total is None else total + part
    return total.reshape(blocks, rows, cols)


def other_kernel(core_ref, got_ref, out_ref):
    for yo in range(2):
        out_ref[:, yo] = products(got_ref, yo, 1 - core_ref[0]).astype(BF16)


def own_kernel(core_ref, got_ref, own_ref):
    for yo in range(2):
        own_ref[:, yo] = products(got_ref, yo, core_ref[0])


def sum_kernel(own_ref, other_ref, *out_refs):
    for at, out_ref in enumerate(out_refs):
        lanes = pl.ds(at * 128, 128)
        summed = own_ref[:, :, :, lanes] + other_ref[:, :, :, lanes].astype(F32)
        out_ref[...] = summed.astype(BF16)


def outgoing(got, core):
    src, depth, cols = got.shape
    got = got.reshape(src // 2, 2, depth, cols)
    tri = (src // 2, 2, depth // 2, cols)
    other = pl.pallas_call(
        other_kernel,
        out_shape=jax.ShapeDtypeStruct(tri, BF16),
        in_specs=[SMEM, VMEM],
        out_specs=VMEM,
        compiler_params=params(),
        name="other",
    )(core, got)
    other = lax.ppermute(other, "core", [(0, 1), (1, 0)])
    own = pl.pallas_call(
        own_kernel,
        out_shape=jax.ShapeDtypeStruct(tri, F32),
        in_specs=[SMEM, VMEM],
        out_specs=VMEM,
        compiler_params=params(),
        name="own",
    )(core, got)
    summed = pl.pallas_call(
        sum_kernel,
        out_shape=[jax.ShapeDtypeStruct(tri[:3] + (128,), BF16)] * (cols // 128),
        in_specs=[VMEM, VMEM],
        out_specs=[VMEM] * (cols // 128),
        compiler_params=params(),
        name="sum",
    )(own, other)
    return [half.reshape(src, depth // 2, 128) for half in summed]


def columns(left, got_ref, yo):
    blocks, _, depth, cols = got_ref.shape
    rows = depth // 2
    right = got_ref[:, yo, rows:, :].reshape(blocks * rows, cols)
    part = lax.dot_general(
        left.reshape(blocks * rows, cols),
        right,
        (((0,), (0,)), ((), ())),
        preferred_element_type=F32,
    )
    return part.reshape(cols // rows, rows, cols).astype(BF16)


def near_kernel(got_ref, z_ref, w_gate_ref, near_ref, gate_ref, w_t):
    rows = z_ref.shape[0]
    per = near_ref.shape[0] // 2
    for yi in range(2):
        for yo in range(2):
            near_ref[yi * per : yi * per + per, yo] = columns(got_ref[:, yi, :rows, :], got_ref, yo)
    w_t[...] = turned(w_gate_ref[1])
    for r in range(rows):
        gate_ref[r] = sigmoid(dot(w_t[...], norm(z_ref[r].astype(F32)).astype(BF16)))


def far_kernel(core_ref, got_ref, left_ref, near_ref, out_ref):
    per = near_ref.shape[0] // 2
    core = core_ref[0]
    for yi in range(2):
        out_ref[pl.ds((yi * 2 + core) * per, per)] = near_ref[yi * per : yi * per + per]
        for yo in range(2):
            out_ref[pl.ds((yi * 2 + 1 - core) * per, per), yo] = columns(left_ref[:, yi], got_ref, yo)


def incoming(got, core, z, w_gate):
    src, depth, cols = got.shape
    rows, hidden, _ = z.shape
    got = got.reshape(src // 2, 2, depth, cols)
    left = lax.ppermute(got[:, :, : depth // 2], "core", [(0, 1), (1, 0)])
    near, gates = pl.pallas_call(
        near_kernel,
        out_shape=(
            jax.ShapeDtypeStruct((2 * cols // rows, 2, rows, cols), BF16),
            jax.ShapeDtypeStruct((rows, hidden, cols), F32),
        ),
        in_specs=[VMEM, VMEM, VMEM],
        out_specs=(VMEM, VMEM),
        scratch_shapes=[pltpu.VMEM((hidden, hidden), BF16)],
        compiler_params=params(),
        name="near",
    )(got, z, w_gate)
    out = pl.pallas_call(
        far_kernel,
        out_shape=jax.ShapeDtypeStruct((src // 2, 2, depth // 2, cols), BF16),
        in_specs=[SMEM, VMEM, VMEM, VMEM],
        out_specs=VMEM,
        compiler_params=params(),
        name="far",
    )(core, got, left, near)
    return out.reshape(src, depth // 2, cols), gates


def updated(tri, z_ref, gates, w_out_t, r):
    y = norm(tri[r].astype(F32)).astype(BF16)
    return z_ref[r].astype(F32) + gates * dot(w_out_t[...], y)


def middle_kernel(
    a_ref, b_ref, z_ref, w_gate_ref, w_out_ref, w_in_ref, out_ref, z_new_ref, tri, sides, w_out_t, w_in_t, w_gate_t
):
    hidden, rows, _ = a_ref.shape
    w_out_t[...] = turned(w_out_ref[0])
    w_in_t[...] = turned(w_in_ref[1])
    w_gate_t[...] = turned(w_gate_ref[0])
    by_row([a_ref, b_ref], tri)
    for r in range(rows):
        gates = sigmoid(dot(w_gate_t[...], norm(z_ref[r].astype(F32)).astype(BF16)))
        z = updated(tri, z_ref, gates, w_out_t, r).astype(BF16)
        z_new_ref[r] = z
        project(norm(z.astype(F32)).astype(BF16), w_in_t[...], r, sides, hidden)
    by_channel(sides, out_ref)


def middle(halves, z, w_gate, w_out, w_in):
    rows, hidden, cols = z.shape
    return pl.pallas_call(
        middle_kernel,
        out_shape=(
            jax.ShapeDtypeStruct((hidden, 2 * rows, cols), BF16),
            jax.ShapeDtypeStruct((rows, hidden, cols), BF16),
        ),
        in_specs=[VMEM] * 6,
        out_specs=(VMEM, VMEM),
        scratch_shapes=[
            pltpu.VMEM((rows, hidden, cols), BF16),
            pltpu.VMEM((2, rows, hidden, cols), BF16),
            pltpu.VMEM((hidden, hidden), BF16),
            pltpu.VMEM((w_in.shape[2], hidden), BF16),
            pltpu.VMEM((hidden, hidden), BF16),
        ],
        compiler_params=params(),
        name="middle",
    )(*halves, z, w_gate, w_out, w_in)


def last_kernel(tri_ref, z_ref, gate_ref, w_out_ref, out_ref, tri, rows_out, w_out_t, sems):
    w_out_t[...] = turned(w_out_ref[1])
    by_row([tri_ref], tri)
    copies = []
    for r in range(tri_ref.shape[1]):
        rows_out[r] = updated(tri, z_ref, gate_ref[r], w_out_t, r).T.astype(BF16)
        copies.append(pltpu.make_async_copy(rows_out.at[r], out_ref.at[r], sems.at[r]))
        copies[-1].start()
    for copy in copies:
        copy.wait()


def last(tri, z, gates, w_out):
    hidden, rows, cols = tri.shape
    return pl.pallas_call(
        last_kernel,
        out_shape=jax.ShapeDtypeStruct((rows, cols, hidden), BF16),
        in_specs=[VMEM] * 4,
        out_specs=HBM,
        scratch_shapes=[
            pltpu.VMEM((rows, hidden, cols), BF16),
            pltpu.VMEM((rows, cols, hidden), BF16),
            pltpu.VMEM((hidden, hidden), BF16),
            pltpu.SemaphoreType.DMA((rows,)),
        ],
        compiler_params=params(),
        name="last",
    )(tri, z, gates, w_out)


def exchange(blocks):
    return lax.all_to_all(blocks, CHIPS, split_axis=0, concat_axis=0, tiled=True)


def plane_first(a, b):
    both = jnp.concatenate([a, b], axis=2)
    shape = both.shape
    planes = 8
    both = both.reshape(planes, -1, *shape[1:]).swapaxes(0, 1)
    both = lax.all_to_all(both, CHIPS[1:], split_axis=0, concat_axis=0, tiled=True)
    both = both.swapaxes(0, 1)
    both = lax.all_to_all(both, CHIPS[0], split_axis=0, concat_axis=0, tiled=True)
    both = both.reshape(shape)
    return both[:, :, :128], both[:, :, 128:]


def at_once(a, b):
    both = exchange(jnp.concatenate([a, b], axis=2))
    return both[:, :, :128], both[:, :, 128:]


def on_device(pair, w_in, w_gate, w_out):
    core = lax.axis_index("core").reshape(1)
    sent, z = first(core, pair, w_in)
    tri = outgoing(exchange(sent), core)
    tri = lax.cond(core[0] == 0, at_once, plane_first, *tri)
    sent, z = middle(tri, z, w_gate, w_out, w_in)
    tri, gates = incoming(exchange(sent), core, z, w_gate)
    return last(exchange(tri), z, gates, w_out)


def solution(mesh):
    mesh = Mesh(mesh.devices.reshape(8, 4, 2, 2, 2), AXES)
    placed = P(("z", "x", "yl"), ("yh", "core"), None)
    return jax.shard_map(
        on_device, mesh=mesh, in_specs=(placed, P(), P(), P()), out_specs=placed, check_vma=False
    )
```

```python
import jax
import jax.numpy as jnp
from jax import lax
from jax.experimental import pallas as pl
from jax.experimental.pallas import tpu as pltpu
from jax.sharding import Mesh, PartitionSpec as P

AXES = ("z", "x", "yl", "yh", "core")
CHIPS = ("z", "x", "yl", "yh")
F32, BF16 = jnp.float32, jnp.bfloat16
VMEM = pl.BlockSpec(memory_space=pltpu.VMEM)
SMEM = pl.BlockSpec(memory_space=pltpu.SMEM)
HBM = pl.BlockSpec(memory_space=pltpu.HBM)


def params():
    return pltpu.CompilerParams(vmem_limit_bytes=14 * 1024 * 1024)


def sigmoid(v):
    return 0.5 * jnp.tanh(0.5 * v) + 0.5


def norm(v):
    mean = jnp.mean(v, axis=0, keepdims=True)
    centred = v - mean
    var = jnp.mean(centred * centred, axis=0, keepdims=True)
    return centred * lax.rsqrt(var + 1e-05)


def turned(w):
    return w.astype(F32).T.astype(BF16)


def dot(a, b):
    return jnp.dot(a, b, preferred_element_type=F32)


def project(x, w_t, r, sides, hidden):
    proj = dot(w_t, x)
    for side in range(2):
        at = 2 * side * hidden
        gates = sigmoid(proj[at + hidden : at + 2 * hidden])
        sides[side, r] = (gates * proj[at : at + hidden]).astype(BF16)


def by_channel(sides, out_ref):
    _, rows, hidden, cols = sides.shape
    for side in range(2):
        for lane in range(0, cols, 128):
            for c in range(0, hidden, 32):
                block = sides[side, :, c : c + 32, lane : lane + 128]
                out_ref[c : c + 32, side * rows : side * rows + rows, lane : lane + 128] = (
                    jnp.swapaxes(block, 0, 1)
                )


def by_row(tri_refs, tri):
    for at, tri_ref in enumerate(tri_refs):
        hidden, _, cols = tri_ref.shape
        for lane in range(0, cols, 128):
            for c in range(0, hidden, 32):
                block = tri_ref[c : c + 32, :, lane : lane + 128]
                tri[:, c : c + 32, at * cols + lane : at * cols + lane + 128] = jnp.swapaxes(block, 0, 1)


def first_kernel(core_ref, pair_ref, w_in_ref, out_ref, z_ref, sides, w_t):
    rows, _, hidden = pair_ref.shape
    w_t[...] = turned(w_in_ref[0])
    for r in range(rows):
        z = pair_ref[r].astype(F32).T
        z_ref[r] = z.astype(BF16)
        project(norm(z).astype(BF16), w_t[...], r, sides, hidden)
    by_channel(sides, out_ref)


def first(core, pair, w_in):
    rows, cols, hidden = pair.shape
    return pl.pallas_call(
        first_kernel,
        out_shape=(
            jax.ShapeDtypeStruct((hidden, 2 * rows, cols), BF16),
            jax.ShapeDtypeStruct((rows, hidden, cols), BF16),
        ),
        in_specs=[SMEM, VMEM, VMEM],
        out_specs=(VMEM, VMEM),
        scratch_shapes=[
            pltpu.VMEM((2, rows, hidden, cols), BF16),
            pltpu.VMEM((w_in.shape[2], hidden), BF16),
        ],
        compiler_params=params(),
        name="first",
    )(core, pair, w_in)


def products(got_ref, yo, core):
    blocks, _, depth, cols = got_ref.shape
    rows = depth // 2
    per = cols // rows
    total = None
    for yk in range(2):
        a = got_ref[:, yk, :rows, :].reshape(blocks * rows, cols)
        b = got_ref[pl.ds((yo * 2 + core) * per, per), yk, rows:, :].reshape(cols, cols)
        part = lax.dot_general(a, b, (((1,), (1,)), ((), ())), preferred_element_type=F32)
        total = part if total is None else total + part
    return total.reshape(blocks, rows, cols)


def other_kernel(core_ref, got_ref, out_ref):
    for yo in range(2):
        out_ref[:, yo] = products(got_ref, yo, 1 - core_ref[0]).astype(BF16)


def own_kernel(core_ref, got_ref, own_ref):
    for yo in range(2):
        own_ref[:, yo] = products(got_ref, yo, core_ref[0])


def sum_kernel(own_ref, other_ref, *out_refs):
    for at, out_ref in enumerate(out_refs):
        lanes = pl.ds(at * 128, 128)
        summed = own_ref[:, :, :, lanes] + other_ref[:, :, :, lanes].astype(F32)
        out_ref[...] = summed.astype(BF16)


def outgoing(got, core):
    src, depth, cols = got.shape
    got = got.reshape(src // 2, 2, depth, cols)
    tri = (src // 2, 2, depth // 2, cols)
    other = pl.pallas_call(
        other_kernel,
        out_shape=jax.ShapeDtypeStruct(tri, BF16),
        in_specs=[SMEM, VMEM],
        out_specs=VMEM,
        compiler_params=params(),
        name="other",
    )(core, got)
    other = lax.ppermute(other, "core", [(0, 1), (1, 0)])
    own = pl.pallas_call(
        own_kernel,
        out_shape=jax.ShapeDtypeStruct(tri, F32),
        in_specs=[SMEM, VMEM],
        out_specs=VMEM,
        compiler_params=params(),
        name="own",
    )(core, got)
    summed = pl.pallas_call(
        sum_kernel,
        out_shape=[jax.ShapeDtypeStruct(tri[:3] + (128,), BF16)] * (cols // 128),
        in_specs=[VMEM, VMEM],
        out_specs=[VMEM] * (cols // 128),
        compiler_params=params(),
        name="sum",
    )(own, other)
    return [half.reshape(src, depth // 2, 128) for half in summed]


def columns(left, got_ref, yo):
    blocks, _, depth, cols = got_ref.shape
    rows = depth // 2
    right = got_ref[:, yo, rows:, :].reshape(blocks * rows, cols)
    part = lax.dot_general(
        left.reshape(blocks * rows, cols),
        right,
        (((0,), (0,)), ((), ())),
        preferred_element_type=F32,
    )
    return part.reshape(cols // rows, rows, cols).astype(BF16)


def near_kernel(got_ref, z_ref, w_gate_ref, near_ref, gate_ref, w_t):
    rows = z_ref.shape[0]
    per = near_ref.shape[0] // 2
    for yi in range(2):
        for yo in range(2):
            near_ref[yi * per : yi * per + per, yo] = columns(got_ref[:, yi, :rows, :], got_ref, yo)
    w_t[...] = turned(w_gate_ref[1])
    for r in range(rows):
        gate_ref[r] = sigmoid(dot(w_t[...], norm(z_ref[r].astype(F32)).astype(BF16)))


def far_kernel(core_ref, got_ref, left_ref, near_ref, out_ref):
    per = near_ref.shape[0] // 2
    core = core_ref[0]
    for yi in range(2):
        out_ref[pl.ds((yi * 2 + core) * per, per)] = near_ref[yi * per : yi * per + per]
        for yo in range(2):
            out_ref[pl.ds((yi * 2 + 1 - core) * per, per), yo] = columns(left_ref[:, yi], got_ref, yo)


def incoming(got, core, z, w_gate):
    src, depth, cols = got.shape
    rows, hidden, _ = z.shape
    got = got.reshape(src // 2, 2, depth, cols)
    left = lax.ppermute(got[:, :, : depth // 2], "core", [(0, 1), (1, 0)])
    near, gates = pl.pallas_call(
        near_kernel,
        out_shape=(
            jax.ShapeDtypeStruct((2 * cols // rows, 2, rows, cols), BF16),
            jax.ShapeDtypeStruct((rows, hidden, cols), F32),
        ),
        in_specs=[VMEM, VMEM, VMEM],
        out_specs=(VMEM, VMEM),
        scratch_shapes=[pltpu.VMEM((hidden, hidden), BF16)],
        compiler_params=params(),
        name="near",
    )(got, z, w_gate)
    out = pl.pallas_call(
        far_kernel,
        out_shape=jax.ShapeDtypeStruct((src // 2, 2, depth // 2, cols), BF16),
        in_specs=[SMEM, VMEM, VMEM, VMEM],
        out_specs=VMEM,
        compiler_params=params(),
        name="far",
    )(core, got, left, near)
    return out.reshape(src, depth // 2, cols), gates


def updated(tri, z_ref, gates, w_out_t, r):
    y = norm(tri[r].astype(F32)).astype(BF16)
    return z_ref[r].astype(F32) + gates * dot(w_out_t[...], y)


def middle_kernel(
    a_ref, b_ref, z_ref, w_gate_ref, w_out_ref, w_in_ref, out_ref, z_new_ref, tri, sides, w_out_t, w_in_t, w_gate_t
):
    hidden, rows, _ = a_ref.shape
    w_out_t[...] = turned(w_out_ref[0])
    w_in_t[...] = turned(w_in_ref[1])
    w_gate_t[...] = turned(w_gate_ref[0])
    by_row([a_ref, b_ref], tri)
    for r in range(rows):
        gates = sigmoid(dot(w_gate_t[...], norm(z_ref[r].astype(F32)).astype(BF16)))
        z = updated(tri, z_ref, gates, w_out_t, r).astype(BF16)
        z_new_ref[r] = z
        project(norm(z.astype(F32)).astype(BF16), w_in_t[...], r, sides, hidden)
    by_channel(sides, out_ref)


def middle(halves, z, w_gate, w_out, w_in):
    rows, hidden, cols = z.shape
    return pl.pallas_call(
        middle_kernel,
        out_shape=(
            jax.ShapeDtypeStruct((hidden, 2 * rows, cols), BF16),
            jax.ShapeDtypeStruct((rows, hidden, cols), BF16),
        ),
        in_specs=[VMEM] * 6,
        out_specs=(VMEM, VMEM),
        scratch_shapes=[
            pltpu.VMEM((rows, hidden, cols), BF16),
            pltpu.VMEM((2, rows, hidden, cols), BF16),
            pltpu.VMEM((hidden, hidden), BF16),
            pltpu.VMEM((w_in.shape[2], hidden), BF16),
            pltpu.VMEM((hidden, hidden), BF16),
        ],
        compiler_params=params(),
        name="middle",
    )(*halves, z, w_gate, w_out, w_in)


def last_kernel(tri_ref, z_ref, gate_ref, w_out_ref, out_ref, tri, rows_out, w_out_t, sems):
    w_out_t[...] = turned(w_out_ref[1])
    by_row([tri_ref], tri)
    copies = []
    for r in range(tri_ref.shape[1]):
        rows_out[r] = updated(tri, z_ref, gate_ref[r], w_out_t, r).T.astype(BF16)
        copies.append(pltpu.make_async_copy(rows_out.at[r], out_ref.at[r], sems.at[r]))
        copies[-1].start()
    for copy in copies:
        copy.wait()


def last(tri, z, gates, w_out):
    hidden, rows, cols = tri.shape
    return pl.pallas_call(
        last_kernel,
        out_shape=jax.ShapeDtypeStruct((rows, cols, hidden), BF16),
        in_specs=[VMEM] * 4,
        out_specs=HBM,
        scratch_shapes=[
            pltpu.VMEM((rows, hidden, cols), BF16),
            pltpu.VMEM((rows, cols, hidden), BF16),
            pltpu.VMEM((hidden, hidden), BF16),
            pltpu.SemaphoreType.DMA((rows,)),
        ],
        compiler_params=params(),
        name="last",
    )(tri, z, gates, w_out)


def exchange(blocks):
    return lax.all_to_all(blocks, CHIPS, split_axis=0, concat_axis=0, tiled=True)


def along(blocks, first, second):
    shape = blocks.shape
    blocks = blocks.reshape(lax.axis_size(CHIPS[0]), -1, *shape[1:])
    for axes in (first, second):
        if axes == CHIPS[0]:
            blocks = lax.all_to_all(blocks, axes, split_axis=0, concat_axis=0, tiled=True)
        else:
            blocks = blocks.swapaxes(0, 1)
            blocks = lax.all_to_all(blocks, axes, split_axis=0, concat_axis=0, tiled=True)
            blocks = blocks.swapaxes(0, 1)
    return blocks.reshape(shape)


def at_once(a, b):
    both = exchange(jnp.concatenate([a, b], axis=2))
    return both[:, :, :128], both[:, :, 128:]


def plane_first(a, b):
    both = along(jnp.concatenate([a, b], axis=2), CHIPS[1:], CHIPS[0])
    return both[:, :, :128], both[:, :, 128:]


def plane_then_z(blocks):
    return along(blocks, CHIPS[1:], CHIPS[0])


def on_device(pair, w_in, w_gate, w_out):
    core = lax.axis_index("core").reshape(1)
    sent, z = first(core, pair, w_in)
    tri = outgoing(lax.cond(core[0] == 0, exchange, plane_then_z, sent), core)
    tri = lax.cond(core[0] == 0, at_once, plane_first, *tri)
    sent, z = middle(tri, z, w_gate, w_out, w_in)
    tri, gates = incoming(exchange(sent), core, z, w_gate)
    return last(exchange(tri), z, gates, w_out)


def solution(mesh):
    mesh = Mesh(mesh.devices.reshape(8, 4, 2, 2, 2), AXES)
    placed = P(("z", "x", "yl"), ("yh", "core"), None)
    return jax.shard_map(
        on_device, mesh=mesh, in_specs=(placed, P(), P(), P()), out_specs=placed, check_vma=False
    )
```

```python
import jax
import jax.numpy as jnp
from jax import lax
from jax.experimental import pallas as pl
from jax.experimental.pallas import tpu as pltpu
from jax.sharding import Mesh, PartitionSpec as P

AXES = ("z", "x", "yl", "yh", "core")
CHIPS = ("z", "x", "yl", "yh")
F32, BF16 = jnp.float32, jnp.bfloat16
VMEM = pl.BlockSpec(memory_space=pltpu.VMEM)
SMEM = pl.BlockSpec(memory_space=pltpu.SMEM)
HBM = pl.BlockSpec(memory_space=pltpu.HBM)


def params():
    return pltpu.CompilerParams(vmem_limit_bytes=14 * 1024 * 1024)


def sigmoid(v):
    return 0.5 * jnp.tanh(0.5 * v) + 0.5


def norm(v):
    mean = jnp.mean(v, axis=0, keepdims=True)
    centred = v - mean
    var = jnp.mean(centred * centred, axis=0, keepdims=True)
    return centred * lax.rsqrt(var + 1e-05)


def turned(w):
    return w.astype(F32).T.astype(BF16)


def dot(a, b):
    return jnp.dot(a, b, preferred_element_type=F32)


def project(x, w_t, r, sides, hidden):
    proj = dot(w_t, x)
    for side in range(2):
        at = 2 * side * hidden
        gates = sigmoid(proj[at + hidden : at + 2 * hidden])
        sides[side, r] = (gates * proj[at : at + hidden]).astype(BF16)


def by_channel(sides, out_ref):
    _, rows, hidden, cols = sides.shape
    for side in range(2):
        for lane in range(0, cols, 128):
            for c in range(0, hidden, 32):
                block = sides[side, :, c : c + 32, lane : lane + 128]
                out_ref[c : c + 32, side * rows : side * rows + rows, lane : lane + 128] = (
                    jnp.swapaxes(block, 0, 1)
                )


def by_row(tri_refs, tri):
    for at, tri_ref in enumerate(tri_refs):
        hidden, _, cols = tri_ref.shape
        for lane in range(0, cols, 128):
            for c in range(0, hidden, 32):
                block = tri_ref[c : c + 32, :, lane : lane + 128]
                tri[:, c : c + 32, at * cols + lane : at * cols + lane + 128] = jnp.swapaxes(block, 0, 1)


def first_kernel(core_ref, pair_ref, w_in_ref, out_ref, z_ref, sides, w_t):
    rows, _, hidden = pair_ref.shape
    w_t[...] = turned(w_in_ref[0])
    for r in range(rows):
        z = pair_ref[r].astype(F32).T
        z_ref[r] = z.astype(BF16)
        project(norm(z).astype(BF16), w_t[...], r, sides, hidden)
    by_channel(sides, out_ref)


def first(core, pair, w_in):
    rows, cols, hidden = pair.shape
    return pl.pallas_call(
        first_kernel,
        out_shape=(
            jax.ShapeDtypeStruct((hidden, 2 * rows, cols), BF16),
            jax.ShapeDtypeStruct((rows, hidden, cols), BF16),
        ),
        in_specs=[SMEM, VMEM, VMEM],
        out_specs=(VMEM, VMEM),
        scratch_shapes=[
            pltpu.VMEM((2, rows, hidden, cols), BF16),
            pltpu.VMEM((w_in.shape[2], hidden), BF16),
        ],
        compiler_params=params(),
        name="first",
    )(core, pair, w_in)


def products(got_ref, yo, core):
    blocks, _, depth, cols = got_ref.shape
    rows = depth // 2
    per = cols // rows
    total = None
    for yk in range(2):
        a = got_ref[:, yk, :rows, :].reshape(blocks * rows, cols)
        b = got_ref[pl.ds((yo * 2 + core) * per, per), yk, rows:, :].reshape(cols, cols)
        part = lax.dot_general(a, b, (((1,), (1,)), ((), ())), preferred_element_type=F32)
        total = part if total is None else total + part
    return total.reshape(blocks, rows, cols)


def other_kernel(core_ref, got_ref, out_ref):
    for yo in range(2):
        out_ref[:, yo] = products(got_ref, yo, 1 - core_ref[0]).astype(BF16)


def own_kernel(core_ref, got_ref, own_ref):
    for yo in range(2):
        own_ref[:, yo] = products(got_ref, yo, core_ref[0])


def sum_kernel(own_ref, other_ref, *out_refs):
    for at, out_ref in enumerate(out_refs):
        lanes = pl.ds(at * 128, 128)
        summed = own_ref[:, :, :, lanes] + other_ref[:, :, :, lanes].astype(F32)
        out_ref[...] = summed.astype(BF16)


def outgoing(got, core):
    src, depth, cols = got.shape
    got = got.reshape(src // 2, 2, depth, cols)
    tri = (src // 2, 2, depth // 2, cols)
    other = pl.pallas_call(
        other_kernel,
        out_shape=jax.ShapeDtypeStruct(tri, BF16),
        in_specs=[SMEM, VMEM],
        out_specs=VMEM,
        compiler_params=params(),
        name="other",
    )(core, got)
    other = lax.ppermute(other, "core", [(0, 1), (1, 0)])
    own = pl.pallas_call(
        own_kernel,
        out_shape=jax.ShapeDtypeStruct(tri, F32),
        in_specs=[SMEM, VMEM],
        out_specs=VMEM,
        compiler_params=params(),
        name="own",
    )(core, got)
    summed = pl.pallas_call(
        sum_kernel,
        out_shape=[jax.ShapeDtypeStruct(tri[:3] + (128,), BF16)] * (cols // 128),
        in_specs=[VMEM, VMEM],
        out_specs=[VMEM] * (cols // 128),
        compiler_params=params(),
        name="sum",
    )(own, other)
    return [half.reshape(src, depth // 2, 128) for half in summed]


def columns(left, got_ref, yo):
    blocks, _, depth, cols = got_ref.shape
    rows = depth // 2
    right = got_ref[:, yo, rows:, :].reshape(blocks * rows, cols)
    part = lax.dot_general(
        left.reshape(blocks * rows, cols),
        right,
        (((0,), (0,)), ((), ())),
        preferred_element_type=F32,
    )
    return part.reshape(cols // rows, rows, cols).astype(BF16)


def near_kernel(got_ref, z_ref, w_gate_ref, near_ref, gate_ref, w_t):
    rows = z_ref.shape[0]
    per = near_ref.shape[0] // 2
    for yi in range(2):
        for yo in range(2):
            near_ref[yi * per : yi * per + per, yo] = columns(got_ref[:, yi, :rows, :], got_ref, yo)
    w_t[...] = turned(w_gate_ref[1])
    for r in range(rows):
        gate_ref[r] = sigmoid(dot(w_t[...], norm(z_ref[r].astype(F32)).astype(BF16)))


def far_kernel(core_ref, got_ref, left_ref, near_ref, out_ref):
    per = near_ref.shape[0] // 2
    core = core_ref[0]
    for yi in range(2):
        out_ref[pl.ds((yi * 2 + core) * per, per)] = near_ref[yi * per : yi * per + per]
        for yo in range(2):
            out_ref[pl.ds((yi * 2 + 1 - core) * per, per), yo] = columns(left_ref[:, yi], got_ref, yo)


def incoming(got, core, z, w_gate):
    src, depth, cols = got.shape
    rows, hidden, _ = z.shape
    got = got.reshape(src // 2, 2, depth, cols)
    left = lax.ppermute(got[:, :, : depth // 2], "core", [(0, 1), (1, 0)])
    near, gates = pl.pallas_call(
        near_kernel,
        out_shape=(
            jax.ShapeDtypeStruct((2 * cols // rows, 2, rows, cols), BF16),
            jax.ShapeDtypeStruct((rows, hidden, cols), F32),
        ),
        in_specs=[VMEM, VMEM, VMEM],
        out_specs=(VMEM, VMEM),
        scratch_shapes=[pltpu.VMEM((hidden, hidden), BF16)],
        compiler_params=params(),
        name="near",
    )(got, z, w_gate)
    out = pl.pallas_call(
        far_kernel,
        out_shape=jax.ShapeDtypeStruct((src // 2, 2, depth // 2, cols), BF16),
        in_specs=[SMEM, VMEM, VMEM, VMEM],
        out_specs=VMEM,
        compiler_params=params(),
        name="far",
    )(core, got, left, near)
    return out.reshape(src, depth // 2, cols), gates


def updated(tri, z_ref, gates, w_out_t, r):
    y = norm(tri[r].astype(F32)).astype(BF16)
    return z_ref[r].astype(F32) + gates * dot(w_out_t[...], y)


def middle_kernel(
    a_ref, b_ref, z_ref, w_gate_ref, w_out_ref, w_in_ref, out_ref, z_new_ref, tri, sides, w_out_t, w_in_t, w_gate_t
):
    hidden, rows, _ = a_ref.shape
    w_out_t[...] = turned(w_out_ref[0])
    w_in_t[...] = turned(w_in_ref[1])
    w_gate_t[...] = turned(w_gate_ref[0])
    by_row([a_ref, b_ref], tri)
    for r in range(rows):
        gates = sigmoid(dot(w_gate_t[...], norm(z_ref[r].astype(F32)).astype(BF16)))
        z = updated(tri, z_ref, gates, w_out_t, r).astype(BF16)
        z_new_ref[r] = z
        project(norm(z.astype(F32)).astype(BF16), w_in_t[...], r, sides, hidden)
    by_channel(sides, out_ref)


def middle(halves, z, w_gate, w_out, w_in):
    rows, hidden, cols = z.shape
    return pl.pallas_call(
        middle_kernel,
        out_shape=(
            jax.ShapeDtypeStruct((hidden, 2 * rows, cols), BF16),
            jax.ShapeDtypeStruct((rows, hidden, cols), BF16),
        ),
        in_specs=[VMEM] * 6,
        out_specs=(VMEM, VMEM),
        scratch_shapes=[
            pltpu.VMEM((rows, hidden, cols), BF16),
            pltpu.VMEM((2, rows, hidden, cols), BF16),
            pltpu.VMEM((hidden, hidden), BF16),
            pltpu.VMEM((w_in.shape[2], hidden), BF16),
            pltpu.VMEM((hidden, hidden), BF16),
        ],
        compiler_params=params(),
        name="middle",
    )(*halves, z, w_gate, w_out, w_in)


def last_kernel(tri_ref, z_ref, gate_ref, w_out_ref, out_ref, tri, rows_out, w_out_t, sems):
    w_out_t[...] = turned(w_out_ref[1])
    by_row([tri_ref], tri)
    copies = []
    for r in range(tri_ref.shape[1]):
        rows_out[r] = updated(tri, z_ref, gate_ref[r], w_out_t, r).T.astype(BF16)
        copies.append(pltpu.make_async_copy(rows_out.at[r], out_ref.at[r], sems.at[r]))
        copies[-1].start()
    for copy in copies:
        copy.wait()


def last(tri, z, gates, w_out):
    hidden, rows, cols = tri.shape
    return pl.pallas_call(
        last_kernel,
        out_shape=jax.ShapeDtypeStruct((rows, cols, hidden), BF16),
        in_specs=[VMEM] * 4,
        out_specs=HBM,
        scratch_shapes=[
            pltpu.VMEM((rows, hidden, cols), BF16),
            pltpu.VMEM((rows, cols, hidden), BF16),
            pltpu.VMEM((hidden, hidden), BF16),
            pltpu.SemaphoreType.DMA((rows,)),
        ],
        compiler_params=params(),
        name="last",
    )(tri, z, gates, w_out)


def exchange(blocks):
    return lax.all_to_all(blocks, CHIPS, split_axis=0, concat_axis=0, tiled=True)


def along(blocks, first, second):
    shape = blocks.shape
    blocks = blocks.reshape(lax.axis_size(CHIPS[0]), -1, *shape[1:])
    for axes in (first, second):
        if axes == CHIPS[0]:
            blocks = lax.all_to_all(blocks, axes, split_axis=0, concat_axis=0, tiled=True)
        else:
            blocks = blocks.swapaxes(0, 1)
            blocks = lax.all_to_all(blocks, axes, split_axis=0, concat_axis=0, tiled=True)
            blocks = blocks.swapaxes(0, 1)
    return blocks.reshape(shape)


def at_once(a, b):
    both = exchange(jnp.concatenate([a, b], axis=2))
    return both[:, :, :128], both[:, :, 128:]


def plane_first(a, b):
    both = along(jnp.concatenate([a, b], axis=2), CHIPS[1:], CHIPS[0])
    return both[:, :, :128], both[:, :, 128:]


def plane_then_z(blocks):
    return along(blocks, CHIPS[1:], CHIPS[0])


def on_device(pair, w_in, w_gate, w_out):
    core = lax.axis_index("core").reshape(1)
    sent, z = first(core, pair, w_in)
    tri = outgoing(lax.cond(core[0] == 0, exchange, plane_then_z, sent), core)
    tri = lax.cond(core[0] == 0, at_once, plane_first, *tri)
    sent, z = middle(tri, z, w_gate, w_out, w_in)
    tri, gates = incoming(exchange(sent), core, z, w_gate)
    return last(lax.cond(core[0] == 0, exchange, plane_then_z, tri), z, gates, w_out)


def solution(mesh):
    mesh = Mesh(mesh.devices.reshape(8, 4, 2, 2, 2), AXES)
    placed = P(("z", "x", "yl"), ("yh", "core"), None)
    return jax.shard_map(
        on_device, mesh=mesh, in_specs=(placed, P(), P(), P()), out_specs=placed, check_vma=False
    )
```
